32 devices in a mesh: tp: 2 (over x), seq: 16 (over z, y, core).
Axes of the slice: x: 2, y: 2, z: 4, core: 2. Of those that a mesh axis runs over, the one named last changes fastest.
Arguments:
- llama_context: bfloat16 [128, 4096], P(None, 'tp'), may hold values from -6 to 6
- llama_residual: bfloat16 [128, 4096], P(None, 'seq'), may hold values from -6 to 6
- w_attn_out: bfloat16 [4096, 4096], P('tp', 'seq'), may hold values from -0.09375 to 0.09375
- w_caption: bfloat16 [4096, 2560], P('seq', 'tp'), may hold values from -0.09375 to 0.09375
- w_text_kv: bfloat16 [2560, 2, 2048], P(None, None, 'tp'), may hold values from -0.125 to 0.125
- prompt_length: int32 [1], replicated, may hold values from 1 to 128, as said below
- image_query: bfloat16 [2, 4096, 2048], P(None, 'seq', 'tp'), may hold values from -32 to 32
- image_key: bfloat16 [2, 4096, 2048], P(None, 'seq', 'tp'), may hold values from -9 to 9
- image_value: bfloat16 [2, 4096, 2048], P(None, 'seq', 'tp'), may hold values from -6 to 6
Outputs:
- joint_context: bfloat16 [2, 4096, 2048], P(None, 'seq', 'tp')
The draws below stay inside these ranges and needn't reach their ends.
Inputs may be any that keep to these rules, and one draw needn't show every extreme that they name: `prompt_length`: one pair's prompt has all 128 tokens live, every other pair's fewer.
All inputs are finite; a program needn't handle non-finite values.
Results may differ from the reference program's by a relative error of at most 0.039.
Values may be sent and summed in bfloat16 or wider, within the bound.
A program may use at most 192 MiB of HBM per device.

```python
import math
import jax
import jax.numpy as jnp
from jax import lax

DL = 4096
TXT = 128
D = 2560
HEADS = 16
HD = 128
IMG = 4096
PAIRS = 1
N_TP = 2


def draw_prompt_length(key, part):
    base = jax.random.fold_in(key, 777)
    pick_key, length_key = jax.random.split(base, 2)
    full_pair = jax.random.randint(pick_key, (), 0, PAIRS)
    shorter = jax.random.randint(length_key, (PAIRS,), 1, TXT)
    places = jnp.arange(PAIRS, dtype=jnp.int32)
    return jnp.where(places == full_pair, TXT, shorter).astype(jnp.int32)


def attention_pair(key):
    base = jax.random.fold_in(key, 4242)
    first_key, second_key = jax.random.split(base, 2)
    extent = (2, PAIRS * IMG, HEADS * HD)
    queries = jnp.clip(1.4 * jax.random.normal(first_key, extent, jnp.float32), -8.4, 8.4)
    key_rows = jnp.clip(1.4 * jax.random.normal(second_key, extent, jnp.float32), -8.4, 8.4)
    return (queries, key_rows)


def draw_image_query(key, part):
    return attention_pair(key)[0].astype(jnp.bfloat16)


def draw_image_key(key, part):
    return attention_pair(key)[1].astype(jnp.bfloat16)


def shard_levels(key, shape, pieces, low, largest):
    loudness = 1.0
    for dim, shards_of in pieces:
        draws = jax.random.uniform(jax.random.fold_in(jax.random.fold_in(key, 6), dim), (shards_of,), jnp.float32, low / len(pieces), largest / len(pieces))
        loudness = loudness * jnp.repeat(jnp.exp(draws), shape[dim] // shards_of).reshape((-1,) + (1,) * (len(shape) - 1 - dim))
    return loudness


def centred(own_key, dims, deviation, reach, cuts=(), kind=jnp.bfloat16):
    array = jax.random.normal(own_key, dims, jnp.float32) * deviation
    if len(cuts) > 0:
        array = shard_levels(own_key, dims, cuts, -0.22, 0.18) * array
    return jnp.clip(array, min=-reach, max=reach).astype(kind)


def setup_inputs(seed: int = 0) -> dict:
    streams_of = jax.random.split(jax.random.key(seed), 10)
    return {
        "llama_context": centred(streams_of[0], (PAIRS * TXT, DL), 1.0, 6.0, ((1, 2),)),
        "llama_residual": centred(streams_of[1], (PAIRS * TXT, DL), 1.0, 6.0, ((1, 16),)),
        "w_attn_out": centred(streams_of[2], (DL, DL), DL ** -0.5, 0.09375, ((0, 2), (1, 16))),
        "w_caption": centred(streams_of[3], (DL, D), DL ** -0.5, 0.09375, ((0, 16), (1, 2))),
        "w_text_kv": centred(streams_of[4], (D, 2, HEADS * HD), D ** -0.5, 0.125, ((2, 2),)),
        "prompt_length": draw_prompt_length(jax.random.fold_in(streams_of[9], 71), 0),
        "image_query": draw_image_query(jax.random.fold_in(streams_of[9], 71), 0),
        "image_key": draw_image_key(jax.random.fold_in(streams_of[9], 71), 0),
        "image_value": centred(streams_of[8], (2, PAIRS * IMG, HEADS * HD), 1.0, 6.0, ((1, 16), (2, 2))),
    }


def blocked_sum(left, right, groups):
    block_width = left.shape[1] // groups
    summed = jnp.zeros((left.shape[0], right.shape[1]), jnp.float32)
    for tp_group in range(groups):
        lower_edge = tp_group * block_width
        partial_term = jnp.dot(left[:, lower_edge:lower_edge + block_width], right[lower_edge:lower_edge + block_width], preferred_element_type=jnp.float32)
        rounded = lax.optimization_barrier(partial_term.astype(jnp.bfloat16))
        summed = summed + rounded.astype(jnp.float32)
    return summed

def reference(llama_context, llama_residual, w_attn_out, w_caption, w_text_kv, prompt_length, image_query, image_key, image_value):
    llama_attn = blocked_sum(llama_context, w_attn_out, N_TP)
    llama_hidden = (llama_residual.astype(jnp.float32) + llama_attn).astype(jnp.bfloat16)
    text_states = jnp.dot(llama_hidden, w_caption, preferred_element_type=jnp.float32).astype(jnp.bfloat16)
    text_kv = jnp.einsum('td,djc->tjc', text_states.astype(jnp.float32), w_text_kv.astype(jnp.float32)).astype(jnp.bfloat16)
    scale_factor = 1.0 / math.sqrt(HD)

    def attend(flat_index):
        side_index = flat_index // (PAIRS * HEADS)
        pair_index = flat_index // HEADS % PAIRS
        lead_column = flat_index % HEADS * HD
        anchor = jnp.zeros((), jnp.int32)
        first_row = (pair_index * IMG).astype(jnp.int32)
        queries = lax.dynamic_slice(image_query, (side_index, first_row, lead_column), (1, IMG, HD))[0]
        image_keys = lax.dynamic_slice(image_key, (side_index, first_row, lead_column), (1, IMG, HD))[0]
        image_values = lax.dynamic_slice(image_value, (side_index, first_row, lead_column), (1, IMG, HD))[0]
        text_pair = lax.dynamic_slice(text_kv, ((pair_index * TXT).astype(jnp.int32), anchor, lead_column), (TXT, 2, HD))
        live_text = jnp.arange(TXT, dtype=jnp.int32) < prompt_length[pair_index]
        live_mask = jnp.concatenate([live_text, jnp.ones((IMG,), bool)])
        key_rows = jnp.concatenate([text_pair[:, 0], image_keys], axis=0)
        value_rows = jnp.concatenate([text_pair[:, 1], image_values], axis=0)
        scores = jnp.dot(queries, key_rows.T, preferred_element_type=jnp.float32) * scale_factor
        scores = jnp.where(live_mask[None, :], scores, -1e+30)
        maxima = lax.optimization_barrier(jnp.max(scores, axis=1, keepdims=True))
        weights = jnp.exp(scores - maxima)
        totals = lax.optimization_barrier(jnp.sum(weights, axis=1, keepdims=True))
        mixture = jnp.dot(weights.astype(jnp.bfloat16), value_rows, preferred_element_type=jnp.float32) / totals
        return mixture.astype(jnp.bfloat16)
    heads_out = lax.map(attend, jnp.arange(2 * PAIRS * HEADS, dtype=jnp.int32))
    joint_context = heads_out.reshape(2, PAIRS, HEADS, IMG, HD).transpose(0, 1, 3, 2, 4).reshape(2, PAIRS * IMG, HEADS * HD)
    return joint_context
```

```python
import functools
import math

import jax
import jax.numpy as jnp
from jax import lax
from jax.experimental import pallas as pl
from jax.experimental.pallas import tpu as pltpu
from jax.sharding import PartitionSpec as P

TXT = 128
HD = 128
IMG = 4096
CHUNK = 1024
FACTOR = math.log2(math.e) / math.sqrt(HD)
NT = (((1,), (1,)), ((), ()))


def flip(index, step, count):
    result = 0
    bit = 1
    while bit < count:
        result = result + ((index // bit + step // bit) % 2) * bit
        bit *= 2
    return result


def send_order(count):
    far = list(range(count // 2, count))
    near = list(range(1, count // 2))
    mixed = []
    for place in range(len(far)):
        mixed.append(far[place])
        if place < len(near):
            mixed.append(near[place])
    return mixed


def attend_kernel(
    group,
    sides,
    heads,
    query,
    key,
    value,
    text,
    bias,
    out,
    key_land,
    value_land,
    query_land,
    text_land,
    text_key,
    text_value,
    result,
    own_sem,
    send_sem,
    recv_sem,
):
    units = sides * heads
    rows = query.shape[1]
    query_rows = query_land.shape[1]
    seq_index = lax.axis_index("seq")
    base = seq_index // group * group
    member = seq_index % group

    def unit_of(who):
        unit = who % units
        return unit // heads, unit % heads, who // units

    def columns(head):
        return pl.ds(pl.multiple_of(head * HD, HD), HD)

    barrier = pltpu.get_barrier_semaphore()
    for step in range(1, group):
        pl.semaphore_signal(
            barrier,
            inc=1,
            device_id={"seq": base + flip(member, step, group)},
            device_id_type=pl.DeviceIdType.MESH,
        )
    pl.semaphore_wait(barrier, group - 1)

    def remote(kind, who, source, target):
        return pltpu.make_async_remote_copy(
            src_ref=source,
            dst_ref=target,
            send_sem=send_sem.at[kind, who],
            recv_sem=recv_sem.at[kind, member],
            device_id={"seq": base + who},
            device_id_type=pl.DeviceIdType.MESH,
        )

    def arrival(kind, who, target):
        return pltpu.make_async_remote_copy(
            src_ref=target,
            dst_ref=target,
            send_sem=send_sem.at[kind, who],
            recv_sem=recv_sem.at[kind, who],
            device_id={"seq": base + who},
            device_id_type=pl.DeviceIdType.MESH,
        )

    def sources(who):
        side, head, part = unit_of(who)
        cols = columns(head)
        first = pl.multiple_of(part * query_rows, query_rows)
        return (
            key.at[side, :, cols],
            value.at[side, :, cols],
            query.at[side, pl.ds(first, query_rows), cols],
            text.at[head],
        )

    def landings(who):
        return (
            key_land.at[who, :, pl.ds(0, HD)],
            value_land.at[who, :, pl.ds(0, HD)],
            query_land.at[who],
            text_land.at[who],
        )

    def out_place(who):
        side, head, part = unit_of(who)
        first = pl.multiple_of(part * query_rows, query_rows)
        return out.at[side, pl.ds(first, query_rows), columns(head)]

    mine_from = sources(member)
    mine_to = landings(member)
    own = [
        pltpu.make_async_copy(mine_from[kind], mine_to[kind], own_sem.at[kind]) for kind in range(4)
    ]
    order = send_order(group)
    for step in order:
        who = flip(member, step, group)
        places = sources(who)
        for kind in (3, 0, 1):
            remote(kind, who, places[kind], landings(member)[kind]).start()
    for copy in own:
        copy.start()

    @pl.loop(0, group - 1)
    def _(place):
        who = flip(member, group - 1 - place, group)
        remote(2, who, sources(who)[2], landings(member)[2]).start()

    value_land[:, :, HD:] = jnp.ones((group, rows, HD), jnp.bfloat16)
    text_value[:, HD:] = jnp.ones((TXT, HD), jnp.bfloat16)

    for copy in own:
        copy.wait()
    for step in order:
        who = flip(member, step, group)
        for kind in (3, 0, 1):
            arrival(kind, who, landings(who)[kind]).wait_recv()

    @pl.loop(0, group)
    def _(who):
        key_land[who, :, HD:] = key_land[who, :, :HD]

    pieces = text_land[...]
    text_keys = pieces[:, 0].reshape(TXT, HD).astype(jnp.bfloat16)
    text_key[:, :HD] = text_keys
    text_key[:, HD:] = text_keys
    text_value[:, :HD] = pieces[:, 1].reshape(TXT, HD).astype(jnp.bfloat16)

    blocks = CHUNK // rows

    @pl.loop(0, group)
    def _(place):
        step = group - 1 - place
        who = flip(member, step, group)

        @pl.when(step > 0)
        def _():
            arrival(2, who, landings(who)[2]).wait_recv()

        scaled = query_land[who].astype(jnp.float32) * FACTOR
        high = scaled.astype(jnp.bfloat16)
        low = (scaled - high.astype(jnp.float32)).astype(jnp.bfloat16)
        pair = jnp.concatenate([high, low], axis=1)
        scores = lax.dot_general(pair, text_key[...], NT, preferred_element_type=jnp.float32)
        scores = scores + bias[...]
        top = jnp.max(scores, axis=1, keepdims=True)
        weights = jnp.exp2(scores - top).astype(jnp.bfloat16)
        total = jnp.dot(weights, text_value[...], preferred_element_type=jnp.float32)
        for first in range(0, group, blocks):
            keys = key_land[first : first + blocks].reshape(CHUNK, 2 * HD)
            values = value_land[first : first + blocks].reshape(CHUNK, 2 * HD)
            scores = lax.dot_general(pair, keys, NT, preferred_element_type=jnp.float32)
            new_top = jnp.maximum(top, jnp.max(scores, axis=1, keepdims=True))
            weights = jnp.exp2(scores - new_top).astype(jnp.bfloat16)
            total = total * jnp.exp2(top - new_top) + jnp.dot(
                weights, values, preferred_element_type=jnp.float32
            )
            top = new_top
        result[who] = (total[:, :HD] / total[:, HD:]).astype(jnp.bfloat16)

        @pl.when(step > 0)
        def _():
            remote(4, who, result.at[who], out_place(member)).start()

        @pl.when(step == 0)
        def _():
            pltpu.make_async_copy(result.at[who], out_place(member), own_sem.at[4]).start()

    pltpu.make_async_copy(result.at[member], out_place(member), own_sem.at[4]).wait()
    for step in order:
        who = flip(member, step, group)
        arrival(4, who, out_place(who)).wait_recv()
        places = sources(who)
        for kind in range(4):
            remote(kind, who, places[kind], landings(member)[kind]).wait_send()
        remote(4, who, result.at[who], out_place(member)).wait_send()


def attend(query, key, value, text, bias):
    sides, rows, width = query.shape
    heads = width // HD
    group = IMG // rows
    units = sides * heads
    assert group % units == 0 and CHUNK % rows == 0
    query_rows = rows * units // group
    kinds = 5
    whole = pl.BlockSpec(memory_space=pl.ANY)
    vmem = pl.BlockSpec(memory_space=pltpu.VMEM)
    return pl.pallas_call(
        functools.partial(attend_kernel, group, sides, heads),
        out_shape=jax.ShapeDtypeStruct(query.shape, jnp.bfloat16),
        in_specs=[whole, whole, whole, vmem, vmem],
        out_specs=whole,
        scratch_shapes=[
            pltpu.VMEM((group, rows, 2 * HD), jnp.bfloat16),
            pltpu.VMEM((group, rows, 2 * HD), jnp.bfloat16),
            pltpu.VMEM((group, query_rows, HD), jnp.bfloat16),
            pltpu.VMEM((group,) + text.shape[1:], jnp.float32),
            pltpu.VMEM((TXT, 2 * HD), jnp.bfloat16),
            pltpu.VMEM((TXT, 2 * HD), jnp.bfloat16),
            pltpu.VMEM((group, query_rows, HD), jnp.bfloat16),
            pltpu.SemaphoreType.DMA((kinds,)),
            pltpu.SemaphoreType.DMA((kinds, group)),
            pltpu.SemaphoreType.DMA((kinds, group)),
        ],
        compiler_params=pltpu.CompilerParams(
            collective_id=0, has_side_effects=True, vmem_limit_bytes=48 * 2**20
        ),
        cost_estimate=pl.CostEstimate(
            flops=8 * query.size * (IMG + TXT),
            bytes_accessed=4 * query.size * 2,
            transcendentals=group * query_rows * (IMG + TXT),
        ),
    )(query, key, value, text, bias)


def local(
    llama_context,
    llama_residual,
    w_attn_out,
    w_caption,
    w_text_kv,
    prompt_length,
    image_query,
    image_key,
    image_value,
):
    llama_term = jnp.dot(llama_context, w_attn_out, preferred_element_type=jnp.float32)
    llama_attn = lax.psum(llama_term.astype(jnp.bfloat16), "tp").astype(jnp.float32)
    llama_hidden = (llama_residual.astype(jnp.float32) + llama_attn).astype(jnp.bfloat16)
    seq_index = lax.axis_index("seq")
    side_count, row_count, local_width = image_query.shape
    group_size = IMG // row_count
    text_rows = TXT // group_size
    text_part = lax.psum_scatter(
        jnp.dot(llama_hidden, w_caption, preferred_element_type=jnp.float32),
        "seq",
        scatter_dimension=0,
        tiled=True,
    )
    text_states = lax.all_gather(text_part.astype(jnp.bfloat16), "tp", axis=1, tiled=True)
    text_kv = jnp.einsum(
        "td,djc->tjc", text_states, w_text_kv, preferred_element_type=jnp.float32
    ).astype(jnp.bfloat16)
    text = text_kv.reshape(text_rows, 2, local_width // HD, HD).transpose(2, 1, 0, 3)
    pair_index = seq_index // group_size
    pair_count = prompt_length.shape[0]
    live_length = jnp.sum(
        jnp.where(jnp.arange(pair_count, dtype=jnp.int32) == pair_index, prompt_length, 0)
    )
    bias = jnp.where(jnp.arange(TXT, dtype=jnp.int32) < live_length, 0.0, -1e30)
    return attend(
        image_query,
        image_key,
        image_value,
        text.astype(jnp.float32),
        bias.astype(jnp.float32)[None, :],
    )


def solution(mesh):
    placed = (
        P(None, "tp"),
        P(None, "seq"),
        P("tp", "seq"),
        P("seq", "tp"),
        P(None, None, "tp"),
        P(),
        P(None, "seq", "tp"),
        P(None, "seq", "tp"),
        P(None, "seq", "tp"),
    )
    return jax.shard_map(
        local, mesh=mesh, in_specs=placed, out_specs=P(None, "seq", "tp"), check_vma=False
    )
```

```python
import functools
import math

import jax
import jax.numpy as jnp
from jax import lax
from jax.experimental import pallas as pl
from jax.experimental.pallas import tpu as pltpu
from jax.sharding import PartitionSpec as P

TXT = 128
HD = 128
IMG = 4096
CHUNK = 1024
FACTOR = math.log2(math.e) / math.sqrt(HD)
NT = (((1,), (1,)), ((), ()))


def flip(index, step, count):
    result = 0
    bit = 1
    while bit < count:
        result = result + ((index // bit + step // bit) % 2) * bit
        bit *= 2
    return result


def mixed_step(place, count):
    odd = place % 2
    return (1 - odd) * (count // 2 + place // 2) + odd * ((place + 1) // 2)


def attend_kernel(
    group,
    sides,
    heads,
    seq_count,
    tp_count,
    query,
    key,
    value,
    context,
    residual,
    w_out,
    w_caption,
    w_head,
    bias,
    out,
    key_land,
    value_land,
    query_land,
    terms,
    parts,
    parts_land,
    states,
    text_key,
    text_value,
    result,
    own_sem,
    send_sem,
    recv_sem,
    term_send,
    term_recv,
    part_send,
    part_recv,
    state_send,
    state_recv,
    side_send,
    side_recv,
):
    units = sides * heads
    rows = query.shape[1]
    query_rows = query_land.shape[1]
    seq_index = lax.axis_index("seq")
    tp_index = lax.axis_index("tp")
    base = seq_index // group * group
    member = seq_index % group

    def unit_of(who):
        unit = who % units
        return unit // heads, unit % heads, who // units

    def columns(head):
        return pl.ds(pl.multiple_of(head * HD, HD), HD)

    barrier = pltpu.get_barrier_semaphore()

    @pl.loop(1, seq_count)
    def _(step):
        pl.semaphore_signal(
            barrier,
            inc=1,
            device_id={"seq": flip(seq_index, step, seq_count)},
            device_id_type=pl.DeviceIdType.MESH,
        )

    for step in range(1, tp_count):
        pl.semaphore_signal(
            barrier,
            inc=1,
            device_id={"tp": flip(tp_index, step, tp_count)},
            device_id_type=pl.DeviceIdType.MESH,
        )
    pl.semaphore_wait(barrier, seq_count + tp_count - 2)

    def transfer(axis, who, source, target, sent, landed):
        return pltpu.make_async_remote_copy(
            src_ref=source,
            dst_ref=target,
            send_sem=sent,
            recv_sem=landed,
            device_id={axis: who},
            device_id_type=pl.DeviceIdType.MESH,
        )

    def remote(kind, who, source, target):
        return pltpu.make_async_remote_copy(
            src_ref=source,
            dst_ref=target,
            send_sem=send_sem.at[kind, who],
            recv_sem=recv_sem.at[kind, member],
            device_id={"seq": base + who},
            device_id_type=pl.DeviceIdType.MESH,
        )

    def arrival(kind, who, target):
        return pltpu.make_async_remote_copy(
            src_ref=target,
            dst_ref=target,
            send_sem=send_sem.at[kind, who],
            recv_sem=recv_sem.at[kind, who],
            device_id={"seq": base + who},
            device_id_type=pl.DeviceIdType.MESH,
        )

    def sources(who):
        side, head, part = unit_of(who)
        cols = columns(head)
        first = pl.multiple_of(part * query_rows, query_rows)
        return (
            key.at[side, :, cols],
            value.at[side, :, cols],
            query.at[side, pl.ds(first, query_rows), cols],
        )

    def landings(who):
        return (
            key_land.at[who, :, pl.ds(0, HD)],
            value_land.at[who, :, pl.ds(0, HD)],
            query_land.at[who],
        )

    def out_place(who):
        side, head, part = unit_of(who)
        first = pl.multiple_of(part * query_rows, query_rows)
        return out.at[side, pl.ds(first, query_rows), columns(head)]

    mine_from = sources(member)
    mine_to = landings(member)
    own = [
        pltpu.make_async_copy(mine_from[kind], mine_to[kind], own_sem.at[kind]) for kind in range(3)
    ]
    def send(kind, step):
        who = flip(member, step, group)
        remote(kind, who, sources(who)[kind], landings(member)[kind]).start()

    def wave(kind, first, last):
        @pl.loop(first, last)
        def _(place):
            send(kind, mixed_step(place, group))

    half = group // 2
    wave(0, 0, half)
    for copy in own:
        copy.start()

    term = jnp.dot(context[...], w_out[...], preferred_element_type=jnp.float32)
    terms[tp_index] = term.astype(jnp.bfloat16)
    for step in range(1, tp_count):
        other = flip(tp_index, step, tp_count)
        mine = terms.at[tp_index]
        transfer("tp", other, mine, mine, term_send.at[other], term_recv.at[tp_index]).start()
    wave(0, half, group - 1)
    value_land[:, :, HD:] = jnp.ones((group, rows, HD), jnp.bfloat16)
    text_value[:, HD:] = jnp.ones((TXT, HD), jnp.bfloat16)
    for step in range(1, tp_count):
        other = flip(tp_index, step, tp_count)
        theirs = terms.at[other]
        transfer("tp", other, theirs, theirs, term_send.at[other], term_recv.at[other]).wait_recv()
    attended = terms[0].astype(jnp.float32)
    for index in range(1, tp_count):
        attended = attended + terms[index].astype(jnp.float32)
    hidden = (residual[...].astype(jnp.float32) + attended).astype(jnp.bfloat16)
    caption = jnp.dot(hidden, w_caption[...], preferred_element_type=jnp.float32)
    parts[...] = caption.reshape(parts.shape).astype(jnp.bfloat16)

    def part_copy(who, landed):
        return transfer(
            "seq",
            who,
            parts.at[who],
            parts_land.at[landed],
            part_send.at[who],
            part_recv.at[landed],
        )

    @pl.loop(1, seq_count)
    def _(step):
        part_copy(flip(seq_index, seq_count - step, seq_count), seq_index).start()

    parts_land[seq_index] = parts[seq_index]
    wave(1, 0, half)

    @pl.loop(1, seq_count)
    def _(step):
        who = flip(seq_index, seq_count - step, seq_count)
        part_copy(who, who).wait_recv()

    summed = jnp.sum(parts_land[...].astype(jnp.float32), axis=0)
    states[tp_index, member] = summed.astype(jnp.bfloat16)

    def state_copy(who, owner):
        place = states.at[tp_index, owner]
        return transfer(
            "seq", base + who, place, place, state_send.at[who], state_recv.at[owner]
        )

    @pl.loop(1, group)
    def _(step):
        state_copy(flip(member, group - step, group), member).start()

    wave(1, half, group - 1)

    @pl.loop(1, group)
    def _(step):
        who = flip(member, group - step, group)
        state_copy(who, who).wait_recv()

    for step in range(1, tp_count):
        other = flip(tp_index, step, tp_count)
        mine = states.at[tp_index]
        transfer("tp", other, mine, mine, side_send.at[other], side_recv.at[tp_index]).start()

    @pl.loop(0, group - 1)
    def _(place):
        send(2, group - 1 - place)

    for step in range(1, tp_count):
        other = flip(tp_index, step, tp_count)
        theirs = states.at[other]
        transfer("tp", other, theirs, theirs, side_send.at[other], side_recv.at[other]).wait_recv()
    depth = w_caption.shape[1]
    text = jnp.zeros((TXT, 2 * HD), jnp.float32)
    for index in range(tp_count):
        block = states[index].astype(jnp.float32).reshape(TXT, depth).astype(jnp.bfloat16)
        text = text + jnp.dot(
            block,
            w_head[index * depth : (index + 1) * depth],
            preferred_element_type=jnp.float32,
        )
    text = text.astype(jnp.bfloat16)
    text_key[:, :HD] = text[:, :HD]
    text_key[:, HD:] = text[:, :HD]
    text_value[:, :HD] = text[:, HD:]

    for copy in own:
        copy.wait()

    @pl.loop(0, group - 1)
    def _(place):
        who = flip(member, mixed_step(place, group), group)
        for kind in range(2):
            arrival(kind, who, landings(who)[kind]).wait_recv()

    @pl.loop(0, group)
    def _(who):
        key_land[who, :, HD:] = key_land[who, :, :HD]

    blocks = CHUNK // rows

    @pl.loop(0, group)
    def _(place):
        step = group - 1 - place
        who = flip(member, step, group)

        @pl.when(step > 0)
        def _():
            arrival(2, who, landings(who)[2]).wait_recv()

        scaled = query_land[who].astype(jnp.float32) * FACTOR
        high = scaled.astype(jnp.bfloat16)
        low = (scaled - high.astype(jnp.float32)).astype(jnp.bfloat16)
        pair = jnp.concatenate([high, low], axis=1)
        scores = lax.dot_general(pair, text_key[...], NT, preferred_element_type=jnp.float32)
        scores = scores + bias[...]
        top = jnp.max(scores, axis=1, keepdims=True)
        weights = jnp.exp2(scores - top).astype(jnp.bfloat16)
        total = jnp.dot(weights, text_value[...], preferred_element_type=jnp.float32)
        for first in range(0, group, blocks):
            keys = key_land[first : first + blocks].reshape(CHUNK, 2 * HD)
            values = value_land[first : first + blocks].reshape(CHUNK, 2 * HD)
            scores = lax.dot_general(pair, keys, NT, preferred_element_type=jnp.float32)
            new_top = jnp.maximum(top, jnp.max(scores, axis=1, keepdims=True))
            weights = jnp.exp2(scores - new_top).astype(jnp.bfloat16)
            total = total * jnp.exp2(top - new_top) + jnp.dot(
                weights, values, preferred_element_type=jnp.float32
            )
            top = new_top
        result[who] = (total[:, :HD] / total[:, HD:]).astype(jnp.bfloat16)

        @pl.when(step > 0)
        def _():
            remote(3, who, result.at[who], out_place(member)).start()

        @pl.when(step == 0)
        def _():
            pltpu.make_async_copy(result.at[who], out_place(member), own_sem.at[3]).start()

    pltpu.make_async_copy(result.at[member], out_place(member), own_sem.at[3]).wait()

    @pl.loop(1, group)
    def _(step):
        who = flip(member, group - step, group)
        arrival(3, who, out_place(who)).wait_recv()
        places = sources(who)
        for kind in range(3):
            remote(kind, who, places[kind], landings(member)[kind]).wait_send()
        remote(3, who, result.at[who], out_place(member)).wait_send()
        state_copy(who, member).wait_send()

    @pl.loop(1, seq_count)
    def _(step):
        part_copy(flip(seq_index, seq_count - step, seq_count), seq_index).wait_send()

    for step in range(1, tp_count):
        other = flip(tp_index, step, tp_count)
        mine = terms.at[tp_index]
        transfer("tp", other, mine, mine, term_send.at[other], term_recv.at[tp_index]).wait_send()
        mine = states.at[tp_index]
        transfer("tp", other, mine, mine, side_send.at[other], side_recv.at[tp_index]).wait_send()


def local(
    llama_context,
    llama_residual,
    w_attn_out,
    w_caption,
    w_text_kv,
    prompt_length,
    image_query,
    image_key,
    image_value,
):
    sides, rows, width = image_query.shape
    heads = width // HD
    group = IMG // rows
    units = sides * heads
    seq_count = lax.axis_size("seq")
    tp_count = lax.axis_size("tp")
    seq_index = lax.axis_index("seq")
    assert group % units == 0 and CHUNK % rows == 0
    query_rows = rows * units // group
    text_rows = TXT // group
    all_rows, features = llama_residual.shape
    depth = w_caption.shape[1]
    pair_index = seq_index // group
    pair_count = prompt_length.shape[0]
    live_length = jnp.sum(
        jnp.where(jnp.arange(pair_count, dtype=jnp.int32) == pair_index, prompt_length, 0)
    )
    bias = jnp.where(jnp.arange(TXT, dtype=jnp.int32) < live_length, 0.0, -1e30)
    head = seq_index % group % units % heads
    w_head = lax.dynamic_slice_in_dim(w_text_kv, head * HD, HD, axis=2)
    kinds = 4
    whole = pl.BlockSpec(memory_space=pl.ANY)
    vmem = pl.BlockSpec(memory_space=pltpu.VMEM)
    return pl.pallas_call(
        functools.partial(attend_kernel, group, sides, heads, seq_count, tp_count),
        out_shape=jax.ShapeDtypeStruct(image_query.shape, jnp.bfloat16),
        in_specs=[whole] * 3 + [vmem] * 6,
        out_specs=whole,
        scratch_shapes=[
            pltpu.VMEM((group, rows, 2 * HD), jnp.bfloat16),
            pltpu.VMEM((group, rows, 2 * HD), jnp.bfloat16),
            pltpu.VMEM((group, query_rows, HD), jnp.bfloat16),
            pltpu.VMEM((tp_count, all_rows, features), jnp.bfloat16),
            pltpu.VMEM((seq_count, text_rows, depth), jnp.bfloat16),
            pltpu.VMEM((seq_count, text_rows, depth), jnp.bfloat16),
            pltpu.VMEM((tp_count, group, text_rows, depth), jnp.bfloat16),
            pltpu.VMEM((TXT, 2 * HD), jnp.bfloat16),
            pltpu.VMEM((TXT, 2 * HD), jnp.bfloat16),
            pltpu.VMEM((group, query_rows, HD), jnp.bfloat16),
            pltpu.SemaphoreType.DMA((kinds,)),
            pltpu.SemaphoreType.DMA((kinds, group)),
            pltpu.SemaphoreType.DMA((kinds, group)),
            pltpu.SemaphoreType.DMA((tp_count,)),
            pltpu.SemaphoreType.DMA((tp_count,)),
            pltpu.SemaphoreType.DMA((seq_count,)),
            pltpu.SemaphoreType.DMA((seq_count,)),
            pltpu.SemaphoreType.DMA((group,)),
            pltpu.SemaphoreType.DMA((group,)),
            pltpu.SemaphoreType.DMA((tp_count,)),
            pltpu.SemaphoreType.DMA((tp_count,)),
        ],
        compiler_params=pltpu.CompilerParams(
            collective_id=0, has_side_effects=True, vmem_limit_bytes=48 * 2**20
        ),
        cost_estimate=pl.CostEstimate(
            flops=8 * image_query.size * (IMG + TXT),
            bytes_accessed=8 * image_query.size,
            transcendentals=group * query_rows * (IMG + TXT),
        ),
    )(
        image_query,
        image_key,
        image_value,
        llama_context,
        llama_residual,
        w_attn_out,
        w_caption,
        w_head.reshape(w_head.shape[0], 2 * HD),
        bias.astype(jnp.float32)[None, :],
    )


def solution(mesh):
    placed = (
        P(None, "tp"),
        P(None, "seq"),
        P("tp", "seq"),
        P("seq", "tp"),
        P(None, None, "tp"),
        P(),
        P(None, "seq", "tp"),
        P(None, "seq", "tp"),
        P(None, "seq", "tp"),
    )
    return jax.shard_map(
        local, mesh=mesh, in_specs=placed, out_specs=P(None, "seq", "tp"), check_vma=False
    )
```

```python
import functools
import math

import jax
import jax.numpy as jnp
from jax import lax
from jax.experimental import pallas as pl
from jax.experimental.pallas import tpu as pltpu
from jax.sharding import PartitionSpec as P

TXT = 128
HD = 128
IMG = 4096
CHUNK = 1024
FACTOR = math.log2(math.e) / math.sqrt(HD)
NT = (((1,), (1,)), ((), ()))


def flip(index, step, count):
    result = 0
    bit = 1
    while bit < count:
        result = result + ((index // bit + step // bit) % 2) * bit
        bit *= 2
    return result


def mixed_step(place, count):
    odd = place % 2
    return (1 - odd) * (count // 2 + place // 2) + odd * ((place + 1) // 2)


def attend_kernel(
    group,
    sides,
    heads,
    seq_count,
    tp_count,
    query,
    key,
    value,
    context_far,
    residual_far,
    w_out_far,
    w_caption_far,
    w_text_far,
    bias,
    out,
    context,
    residual,
    w_out,
    w_caption,
    w_head,
    key_land,
    value_land,
    query_land,
    terms,
    parts,
    chip_land,
    chip_parts,
    parts_land,
    states,
    text_key,
    text_value,
    result,
    load_sem,
    core_sem,
    own_sem,
    send_sem,
    recv_sem,
    term_send,
    term_recv,
    part_send,
    part_recv,
    state_send,
    state_recv,
    side_send,
    side_recv,
):
    units = sides * heads
    rows = query.shape[1]
    query_rows = query_land.shape[1]
    seq_index = lax.axis_index("seq")
    tp_index = lax.axis_index("tp")
    base = seq_index // group * group
    member = seq_index % group

    def unit_of(who):
        unit = who % units
        return unit // heads, unit % heads, who // units

    def columns(head):
        return pl.ds(pl.multiple_of(head * HD, HD), HD)

    core = seq_index % 2
    twin = flip(seq_index, 1, seq_count)
    chip = seq_index // 2
    chips = seq_count // 2
    head_here = unit_of(member)[1]
    loads = [
        pltpu.make_async_copy(source, target, load_sem.at[index])
        for index, (source, target) in enumerate(
            (
                (context_far, context),
                (w_out_far, w_out),
                (residual_far, residual),
                (w_caption_far, w_caption),
                (w_text_far.at[:, :, columns(head_here)], w_head),
            )
        )
    ]
    for load in loads:
        load.start()

    barrier = pltpu.get_barrier_semaphore()

    @pl.loop(1, seq_count)
    def _(step):
        pl.semaphore_signal(
            barrier,
            inc=1,
            device_id={"seq": flip(seq_index, step, seq_count)},
            device_id_type=pl.DeviceIdType.MESH,
        )

    for step in range(1, tp_count):
        pl.semaphore_signal(
            barrier,
            inc=1,
            device_id={"tp": flip(tp_index, step, tp_count)},
            device_id_type=pl.DeviceIdType.MESH,
        )
    pl.semaphore_wait(barrier, seq_count + tp_count - 2)

    def transfer(axis, who, source, target, sent, landed):
        return pltpu.make_async_remote_copy(
            src_ref=source,
            dst_ref=target,
            send_sem=sent,
            recv_sem=landed,
            device_id={axis: who},
            device_id_type=pl.DeviceIdType.MESH,
        )

    def remote(kind, who, source, target):
        return pltpu.make_async_remote_copy(
            src_ref=source,
            dst_ref=target,
            send_sem=send_sem.at[kind, who],
            recv_sem=recv_sem.at[kind, member],
            device_id={"seq": base + who},
            device_id_type=pl.DeviceIdType.MESH,
        )

    def arrival(kind, who, target):
        return pltpu.make_async_remote_copy(
            src_ref=target,
            dst_ref=target,
            send_sem=send_sem.at[kind, who],
            recv_sem=recv_sem.at[kind, who],
            device_id={"seq": base + who},
            device_id_type=pl.DeviceIdType.MESH,
        )

    def sources(who):
        side, head, part = unit_of(who)
        cols = columns(head)
        first = pl.multiple_of(part * query_rows, query_rows)
        return (
            key.at[side, :, cols],
            value.at[side, :, cols],
            query.at[side, pl.ds(first, query_rows), cols],
        )

    def landings(who):
        return (
            key_land.at[who, :, pl.ds(0, HD)],
            value_land.at[who, :, pl.ds(0, HD)],
            query_land.at[who],
        )

    def out_place(who):
        side, head, part = unit_of(who)
        first = pl.multiple_of(part * query_rows, query_rows)
        return out.at[side, pl.ds(first, query_rows), columns(head)]

    mine_from = sources(member)
    mine_to = landings(member)
    own = [
        pltpu.make_async_copy(mine_from[kind], mine_to[kind], own_sem.at[kind]) for kind in range(3)
    ]
    def send(kind, step):
        who = flip(member, step, group)
        remote(kind, who, sources(who)[kind], landings(member)[kind]).start()

    def wave(kind, first, last):
        @pl.loop(first, last)
        def _(place):
            send(kind, mixed_step(place, group))

    half = group // 2
    wave(0, 0, half)
    for copy in own:
        copy.start()

    loads[0].wait()
    loads[1].wait()
    term = jnp.dot(context[...], w_out[...], preferred_element_type=jnp.float32)
    terms[tp_index] = term.astype(jnp.bfloat16)
    for step in range(1, tp_count):
        other = flip(tp_index, step, tp_count)
        mine = terms.at[tp_index]
        transfer("tp", other, mine, mine, term_send.at[other], term_recv.at[tp_index]).start()
    wave(0, half, group - 1)
    value_land[:, :, HD:] = jnp.ones((group, rows, HD), jnp.bfloat16)
    text_value[:, HD:] = jnp.ones((TXT, HD), jnp.bfloat16)
    for step in range(1, tp_count):
        other = flip(tp_index, step, tp_count)
        theirs = terms.at[other]
        transfer("tp", other, theirs, theirs, term_send.at[other], term_recv.at[other]).wait_recv()
    attended = terms[0].astype(jnp.float32)
    for index in range(1, tp_count):
        attended = attended + terms[index].astype(jnp.float32)
    loads[2].wait()
    loads[3].wait()
    hidden = (residual[...].astype(jnp.float32) + attended).astype(jnp.bfloat16)
    caption = jnp.dot(hidden, w_caption[...], preferred_element_type=jnp.float32)
    split = caption.reshape(chips, 2, parts.shape[2], parts.shape[3]).astype(jnp.bfloat16)
    parts[0] = split[:, 0]
    parts[1] = split[:, 1]
    across = transfer(
        "seq", twin, parts.at[1 - core], chip_land, core_sem.at[0], core_sem.at[1]
    )
    across.start()
    wave(1, 0, half // 2)
    across.wait_recv()
    chip_parts[...] = (
        parts[core].astype(jnp.float32) + chip_land[...].astype(jnp.float32)
    ).astype(jnp.bfloat16)

    def part_copy(who, landed):
        return transfer(
            "seq",
            who * 2 + core,
            chip_parts.at[who],
            parts_land.at[landed],
            part_send.at[who],
            part_recv.at[landed],
        )

    @pl.loop(1, chips)
    def _(step):
        part_copy(flip(chip, chips - step, chips), chip).start()

    parts_land[chip] = chip_parts[chip]
    wave(1, half // 2, half)

    @pl.loop(1, chips)
    def _(step):
        who = flip(chip, chips - step, chips)
        part_copy(who, who).wait_recv()

    summed = jnp.sum(parts_land[...].astype(jnp.float32), axis=0)
    place = member // 2
    places_here = group // 2
    states[tp_index, core, place] = summed.astype(jnp.bfloat16)

    def state_copy(who, owner):
        block = states.at[tp_index, core, owner]
        return transfer(
            "seq", base + who * 2 + core, block, block, state_send.at[who], state_recv.at[owner]
        )

    @pl.loop(1, places_here)
    def _(step):
        state_copy(flip(place, places_here - step, places_here), place).start()

    wave(1, half, half + half // 2)

    @pl.loop(1, places_here)
    def _(step):
        who = flip(place, places_here - step, places_here)
        state_copy(who, who).wait_recv()

    def states_across(half_from):
        block = states.at[tp_index, half_from]
        return transfer("seq", twin, block, block, core_sem.at[2], core_sem.at[3])

    states_across(core).start()
    wave(1, half + half // 2, group - 1)
    states_across(1 - core).wait_recv()

    for step in range(1, tp_count):
        other = flip(tp_index, step, tp_count)
        mine = states.at[tp_index]
        transfer("tp", other, mine, mine, side_send.at[other], side_recv.at[tp_index]).start()

    @pl.loop(0, group - 1)
    def _(place):
        send(2, group - 1 - place)

    for step in range(1, tp_count):
        other = flip(tp_index, step, tp_count)
        theirs = states.at[other]
        transfer("tp", other, theirs, theirs, side_send.at[other], side_recv.at[other]).wait_recv()
    depth = w_caption.shape[1]
    loads[4].wait()
    text = [jnp.zeros((TXT, HD), jnp.float32) for _ in range(2)]
    for index in range(tp_count):
        block = states[index].astype(jnp.float32).reshape(TXT, depth).astype(jnp.bfloat16)
        cut = pl.ds(index * depth, depth)
        for kind in range(2):
            text[kind] = text[kind] + jnp.dot(
                block, w_head[cut, kind, :], preferred_element_type=jnp.float32
            )
    text_keys = text[0].astype(jnp.bfloat16)
    text_key[:, :HD] = text_keys
    text_key[:, HD:] = text_keys
    text_value[:, :HD] = text[1].astype(jnp.bfloat16)

    for copy in own:
        copy.wait()

    @pl.loop(0, group - 1)
    def _(place):
        who = flip(member, mixed_step(place, group), group)
        for kind in range(2):
            arrival(kind, who, landings(who)[kind]).wait_recv()

    @pl.loop(0, group)
    def _(who):
        key_land[who, :, HD:] = key_land[who, :, :HD]

    blocks = CHUNK // rows

    @pl.loop(0, group)
    def _(place):
        step = group - 1 - place
        who = flip(member, step, group)

        @pl.when(step > 0)
        def _():
            arrival(2, who, landings(who)[2]).wait_recv()

        scaled = query_land[who].astype(jnp.float32) * FACTOR
        high = scaled.astype(jnp.bfloat16)
        low = (scaled - high.astype(jnp.float32)).astype(jnp.bfloat16)
        pair = jnp.concatenate([high, low], axis=1)
        scores = lax.dot_general(pair, text_key[...], NT, preferred_element_type=jnp.float32)
        scores = scores + bias[...]
        top = jnp.max(scores, axis=1, keepdims=True)
        weights = jnp.exp2(scores - top).astype(jnp.bfloat16)
        total = jnp.dot(weights, text_value[...], preferred_element_type=jnp.float32)
        for first in range(0, group, blocks):
            keys = key_land[first : first + blocks].reshape(CHUNK, 2 * HD)
            values = value_land[first : first + blocks].reshape(CHUNK, 2 * HD)
            scores = lax.dot_general(pair, keys, NT, preferred_element_type=jnp.float32)
            new_top = jnp.maximum(top, jnp.max(scores, axis=1, keepdims=True))
            weights = jnp.exp2(scores - new_top).astype(jnp.bfloat16)
            total = total * jnp.exp2(top - new_top) + jnp.dot(
                weights, values, preferred_element_type=jnp.float32
            )
            top = new_top
        result[who] = (total[:, :HD] / total[:, HD:]).astype(jnp.bfloat16)

        @pl.when(step > 0)
        def _():
            remote(3, who, result.at[who], out_place(member)).start()

        @pl.when(step == 0)
        def _():
            pltpu.make_async_copy(result.at[who], out_place(member), own_sem.at[3]).start()

    pltpu.make_async_copy(result.at[member], out_place(member), own_sem.at[3]).wait()

    @pl.loop(1, group)
    def _(step):
        who = flip(member, group - step, group)
        arrival(3, who, out_place(who)).wait_recv()
        places = sources(who)
        for kind in range(3):
            remote(kind, who, places[kind], landings(member)[kind]).wait_send()
        remote(3, who, result.at[who], out_place(member)).wait_send()

    @pl.loop(1, places_here)
    def _(step):
        state_copy(flip(place, places_here - step, places_here), place).wait_send()

    @pl.loop(1, chips)
    def _(step):
        part_copy(flip(chip, chips - step, chips), chip).wait_send()

    across.wait_send()
    states_across(core).wait_send()

    for step in range(1, tp_count):
        other = flip(tp_index, step, tp_count)
        mine = terms.at[tp_index]
        transfer("tp", other, mine, mine, term_send.at[other], term_recv.at[tp_index]).wait_send()
        mine = states.at[tp_index]
        transfer("tp", other, mine, mine, side_send.at[other], side_recv.at[tp_index]).wait_send()


def local(
    llama_context,
    llama_residual,
    w_attn_out,
    w_caption,
    w_text_kv,
    prompt_length,
    image_query,
    image_key,
    image_value,
):
    sides, rows, width = image_query.shape
    heads = width // HD
    group = IMG // rows
    units = sides * heads
    seq_count = lax.axis_size("seq")
    tp_count = lax.axis_size("tp")
    seq_index = lax.axis_index("seq")
    assert group % units == 0 and CHUNK % rows == 0
    query_rows = rows * units // group
    text_rows = TXT // group
    chips = seq_count // 2
    all_rows, features = llama_residual.shape
    depth = w_caption.shape[1]
    pair_index = seq_index // group
    pair_count = prompt_length.shape[0]
    live_length = jnp.sum(
        jnp.where(jnp.arange(pair_count, dtype=jnp.int32) == pair_index, prompt_length, 0)
    )
    tokens = jnp.arange(TXT, dtype=jnp.int32).reshape(group // 2, 2, text_rows)
    tokens = tokens.transpose(1, 0, 2).reshape(TXT)
    bias = jnp.where(tokens < live_length, 0.0, -1e30)
    kinds = 4
    whole = pl.BlockSpec(memory_space=pl.ANY)
    vmem = pl.BlockSpec(memory_space=pltpu.VMEM)
    return pl.pallas_call(
        functools.partial(attend_kernel, group, sides, heads, seq_count, tp_count),
        out_shape=jax.ShapeDtypeStruct(image_query.shape, jnp.bfloat16),
        in_specs=[whole] * 8 + [vmem],
        out_specs=whole,
        scratch_shapes=[
            pltpu.VMEM(llama_context.shape, jnp.bfloat16),
            pltpu.VMEM(llama_residual.shape, jnp.bfloat16),
            pltpu.VMEM(w_attn_out.shape, jnp.bfloat16),
            pltpu.VMEM(w_caption.shape, jnp.bfloat16),
            pltpu.VMEM(w_text_kv.shape[:2] + (HD,), jnp.bfloat16),
            pltpu.VMEM((group, rows, 2 * HD), jnp.bfloat16),
            pltpu.VMEM((group, rows, 2 * HD), jnp.bfloat16),
            pltpu.VMEM((group, query_rows, HD), jnp.bfloat16),
            pltpu.VMEM((tp_count, all_rows, features), jnp.bfloat16),
            pltpu.VMEM((2, chips, text_rows, depth), jnp.bfloat16),
            pltpu.VMEM((chips, text_rows, depth), jnp.bfloat16),
            pltpu.VMEM((chips, text_rows, depth), jnp.bfloat16),
            pltpu.VMEM((chips, text_rows, depth), jnp.bfloat16),
            pltpu.VMEM((tp_count, 2, group // 2, text_rows, depth), jnp.bfloat16),
            pltpu.VMEM((TXT, 2 * HD), jnp.bfloat16),
            pltpu.VMEM((TXT, 2 * HD), jnp.bfloat16),
            pltpu.VMEM((group, query_rows, HD), jnp.bfloat16),
            pltpu.SemaphoreType.DMA((5,)),
            pltpu.SemaphoreType.DMA((4,)),
            pltpu.SemaphoreType.DMA((kinds,)),
            pltpu.SemaphoreType.DMA((kinds, group)),
            pltpu.SemaphoreType.DMA((kinds, group)),
            pltpu.SemaphoreType.DMA((tp_count,)),
            pltpu.SemaphoreType.DMA((tp_count,)),
            pltpu.SemaphoreType.DMA((chips,)),
            pltpu.SemaphoreType.DMA((chips,)),
            pltpu.SemaphoreType.DMA((group // 2,)),
            pltpu.SemaphoreType.DMA((group // 2,)),
            pltpu.SemaphoreType.DMA((tp_count,)),
            pltpu.SemaphoreType.DMA((tp_count,)),
        ],
        compiler_params=pltpu.CompilerParams(
            collective_id=0, has_side_effects=True, vmem_limit_bytes=48 * 2**20
        ),
        cost_estimate=pl.CostEstimate(
            flops=8 * image_query.size * (IMG + TXT),
            bytes_accessed=8 * image_query.size,
            transcendentals=group * query_rows * (IMG + TXT),
        ),
    )(
        image_query,
        image_key,
        image_value,
        llama_context,
        llama_residual,
        w_attn_out,
        w_caption,
        w_text_kv,
        bias.astype(jnp.float32)[None, :],
    )


def solution(mesh):
    placed = (
        P(None, "tp"),
        P(None, "seq"),
        P("tp", "seq"),
        P("seq", "tp"),
        P(None, None, "tp"),
        P(),
        P(None, "seq", "tp"),
        P(None, "seq", "tp"),
        P(None, "seq", "tp"),
    )
    return jax.shard_map(
        local, mesh=mesh, in_specs=placed, out_specs=P(None, "seq", "tp"), check_vma=False
    )
```

```python
import functools
import math

import jax
import jax.numpy as jnp
from jax import lax
from jax.experimental import pallas as pl
from jax.experimental.pallas import tpu as pltpu
from jax.sharding import PartitionSpec as P

TXT = 128
HD = 128
IMG = 4096
CHUNK = 1024
FACTOR = math.log2(math.e) / math.sqrt(HD)
NT = (((1,), (1,)), ((), ()))


def flip(index, step, count):
    result = 0
    bit = 1
    while bit < count:
        result = result + ((index // bit + step // bit) % 2) * bit
        bit *= 2
    return result


def attend_kernel(
    group,
    sides,
    heads,
    seq_count,
    tp_count,
    query,
    key,
    value,
    context_far,
    residual_far,
    w_out_far,
    w_caption_far,
    w_text_far,
    bias,
    out,
    context,
    residual,
    w_out,
    w_caption,
    w_head,
    key_land,
    value_land,
    query_land,
    terms,
    parts,
    chip_land,
    chip_parts,
    parts_land,
    states,
    text_key,
    text_value,
    result,
    top_kept,
    total_kept,
    load_sem,
    core_sem,
    own_sem,
    send_sem,
    recv_sem,
    term_send,
    term_recv,
    part_send,
    part_recv,
    state_send,
    state_recv,
    side_send,
    side_recv,
):
    units = sides * heads
    rows = query.shape[1]
    query_rows = query_land.shape[1]
    seq_index = lax.axis_index("seq")
    tp_index = lax.axis_index("tp")
    base = seq_index // group * group
    member = seq_index % group

    def unit_of(who):
        unit = who % units
        return unit // heads, unit % heads, who // units

    def columns(head):
        return pl.ds(pl.multiple_of(head * HD, HD), HD)

    core = seq_index % 2
    twin = flip(seq_index, 1, seq_count)
    chip = seq_index // 2
    chips = seq_count // 2
    head_here = unit_of(member)[1]
    loads = [
        pltpu.make_async_copy(source, target, load_sem.at[index])
        for index, (source, target) in enumerate(
            (
                (context_far, context),
                (w_out_far, w_out),
                (residual_far, residual),
                (w_caption_far, w_caption),
                (w_text_far.at[:, :, columns(head_here)], w_head),
            )
        )
    ]
    for load in loads:
        load.start()

    barrier = pltpu.get_barrier_semaphore()

    @pl.loop(1, seq_count)
    def _(step):
        pl.semaphore_signal(
            barrier,
            inc=1,
            device_id={"seq": flip(seq_index, step, seq_count)},
            device_id_type=pl.DeviceIdType.MESH,
        )

    for step in range(1, tp_count):
        pl.semaphore_signal(
            barrier,
            inc=1,
            device_id={"tp": flip(tp_index, step, tp_count)},
            device_id_type=pl.DeviceIdType.MESH,
        )
    pl.semaphore_wait(barrier, seq_count + tp_count - 2)

    def transfer(axis, who, source, target, sent, landed):
        return pltpu.make_async_remote_copy(
            src_ref=source,
            dst_ref=target,
            send_sem=sent,
            recv_sem=landed,
            device_id={axis: who},
            device_id_type=pl.DeviceIdType.MESH,
        )

    def remote(kind, who, source, target):
        return pltpu.make_async_remote_copy(
            src_ref=source,
            dst_ref=target,
            send_sem=send_sem.at[kind, who],
            recv_sem=recv_sem.at[kind, member],
            device_id={"seq": base + who},
            device_id_type=pl.DeviceIdType.MESH,
        )

    def arrival(kind, who, target):
        return pltpu.make_async_remote_copy(
            src_ref=target,
            dst_ref=target,
            send_sem=send_sem.at[kind, who],
            recv_sem=recv_sem.at[kind, who],
            device_id={"seq": base + who},
            device_id_type=pl.DeviceIdType.MESH,
        )

    def sources(who):
        side, head, part = unit_of(who)
        cols = columns(head)
        first = pl.multiple_of(part * query_rows, query_rows)
        return (
            key.at[side, :, cols],
            value.at[side, :, cols],
            query.at[side, pl.ds(first, query_rows), cols],
        )

    def landings(who):
        return (
            key_land.at[who, :, pl.ds(0, HD)],
            value_land.at[who, :, pl.ds(0, HD)],
            query_land.at[who],
        )

    def out_place(who):
        side, head, part = unit_of(who)
        first = pl.multiple_of(part * query_rows, query_rows)
        return out.at[side, pl.ds(first, query_rows), columns(head)]

    mine_from = sources(member)
    mine_to = landings(member)
    own = [
        pltpu.make_async_copy(mine_from[kind], mine_to[kind], own_sem.at[kind]) for kind in range(3)
    ]
    def send(kind, step):
        who = flip(member, step, group)
        remote(kind, who, sources(who)[kind], landings(member)[kind]).start()

    def key_wave(first, last):
        @pl.loop(first, last)
        def _(place):
            send(0, half + place)
            send(0, place + 1)
            send(1, place + 1)

    def value_wave(first, last):
        @pl.loop(first, last)
        def _(place):
            send(1, half + place)
            send(2, place + 1)

    half = group // 2
    key_wave(0, half // 2)
    for copy in own:
        copy.start()

    loads[0].wait()
    loads[1].wait()
    term = jnp.dot(context[...], w_out[...], preferred_element_type=jnp.float32)
    terms[tp_index] = term.astype(jnp.bfloat16)
    for step in range(1, tp_count):
        other = flip(tp_index, step, tp_count)
        mine = terms.at[tp_index]
        transfer("tp", other, mine, mine, term_send.at[other], term_recv.at[tp_index]).start()
    key_wave(half // 2, half - 1)
    send(0, group - 1)
    value_land[:, :, HD:] = jnp.ones((group, rows, HD), jnp.bfloat16)
    text_value[:, HD:] = jnp.ones((TXT, HD), jnp.bfloat16)
    for step in range(1, tp_count):
        other = flip(tp_index, step, tp_count)
        theirs = terms.at[other]
        transfer("tp", other, theirs, theirs, term_send.at[other], term_recv.at[other]).wait_recv()
    attended = terms[0].astype(jnp.float32)
    for index in range(1, tp_count):
        attended = attended + terms[index].astype(jnp.float32)
    loads[2].wait()
    loads[3].wait()
    hidden = (residual[...].astype(jnp.float32) + attended).astype(jnp.bfloat16)
    caption = jnp.dot(hidden, w_caption[...], preferred_element_type=jnp.float32)
    split = caption.reshape(chips, 2, parts.shape[2], parts.shape[3]).astype(jnp.bfloat16)
    parts[0] = split[:, 0]
    parts[1] = split[:, 1]
    across = transfer(
        "seq", twin, parts.at[1 - core], chip_land, core_sem.at[0], core_sem.at[1]
    )
    across.start()
    value_wave(0, half // 4)
    across.wait_recv()
    chip_parts[...] = (
        parts[core].astype(jnp.float32) + chip_land[...].astype(jnp.float32)
    ).astype(jnp.bfloat16)

    def part_copy(who, landed):
        return transfer(
            "seq",
            who * 2 + core,
            chip_parts.at[who],
            parts_land.at[landed],
            part_send.at[who],
            part_recv.at[landed],
        )

    @pl.loop(1, chips)
    def _(step):
        part_copy(flip(chip, chips - step, chips), chip).start()

    parts_land[chip] = chip_parts[chip]
    value_wave(half // 4, half // 2)

    @pl.loop(1, chips)
    def _(step):
        who = flip(chip, chips - step, chips)
        part_copy(who, who).wait_recv()

    summed = jnp.sum(parts_land[...].astype(jnp.float32), axis=0)
    place = member // 2
    places_here = group // 2
    states[tp_index, core, place] = summed.astype(jnp.bfloat16)

    def state_copy(who, owner):
        block = states.at[tp_index, core, owner]
        return transfer(
            "seq", base + who * 2 + core, block, block, state_send.at[who], state_recv.at[owner]
        )

    @pl.loop(1, places_here)
    def _(step):
        state_copy(flip(place, places_here - step, places_here), place).start()

    value_wave(half // 2, half // 2 + half // 4)

    @pl.loop(1, places_here)
    def _(step):
        who = flip(place, places_here - step, places_here)
        state_copy(who, who).wait_recv()

    def states_across(half_from):
        block = states.at[tp_index, half_from]
        return transfer("seq", twin, block, block, core_sem.at[2], core_sem.at[3])

    states_across(core).start()
    value_wave(half // 2 + half // 4, half - 1)
    send(1, group - 1)
    states_across(1 - core).wait_recv()

    for step in range(1, tp_count):
        other = flip(tp_index, step, tp_count)
        mine = states.at[tp_index]
        transfer("tp", other, mine, mine, side_send.at[other], side_recv.at[tp_index]).start()

    @pl.loop(half, group)
    def _(step):
        send(2, step)

    for step in range(1, tp_count):
        other = flip(tp_index, step, tp_count)
        theirs = states.at[other]
        transfer("tp", other, theirs, theirs, side_send.at[other], side_recv.at[other]).wait_recv()
    depth = w_caption.shape[1]
    loads[4].wait()
    text = [jnp.zeros((TXT, HD), jnp.float32) for _ in range(2)]
    for index in range(tp_count):
        block = states[index].astype(jnp.float32).reshape(TXT, depth).astype(jnp.bfloat16)
        cut = pl.ds(index * depth, depth)
        for kind in range(2):
            text[kind] = text[kind] + jnp.dot(
                block, w_head[cut, kind, :], preferred_element_type=jnp.float32
            )
    text_keys = text[0].astype(jnp.bfloat16)
    text_key[:, :HD] = text_keys
    text_key[:, HD:] = text_keys
    text_value[:, :HD] = text[1].astype(jnp.bfloat16)

    for copy in own:
        copy.wait()

    def settle(first_step, last_step):
        @pl.loop(first_step, last_step)
        def _(step):
            who = flip(member, step, group)

            @pl.when(step > 0)
            def _():
                for kind in range(2):
                    arrival(kind, who, landings(who)[kind]).wait_recv()

            key_land[who, :, HD:] = key_land[who, :, :HD]

    def query_pair(who):
        scaled = query_land[who].astype(jnp.float32) * FACTOR
        high = scaled.astype(jnp.bfloat16)
        low = (scaled - high.astype(jnp.float32)).astype(jnp.bfloat16)
        return jnp.concatenate([high, low], axis=1)

    def start_text(pair):
        scores = lax.dot_general(pair, text_key[...], NT, preferred_element_type=jnp.float32)
        scores = scores + bias[...]
        top = jnp.max(scores, axis=1, keepdims=True)
        weights = jnp.exp2(scores - top).astype(jnp.bfloat16)
        return top, jnp.dot(weights, text_value[...], preferred_element_type=jnp.float32)

    blocks = CHUNK // rows

    def absorb(pair, top, total, lead):
        for first in range(0, half, blocks):
            cut = pl.ds(lead + first, blocks)
            keys = key_land[cut].reshape(CHUNK, 2 * HD)
            values = value_land[cut].reshape(CHUNK, 2 * HD)
            scores = lax.dot_general(pair, keys, NT, preferred_element_type=jnp.float32)
            new_top = jnp.maximum(top, jnp.max(scores, axis=1, keepdims=True))
            weights = jnp.exp2(scores - new_top).astype(jnp.bfloat16)
            total = total * jnp.exp2(top - new_top) + jnp.dot(
                weights, values, preferred_element_type=jnp.float32
            )
            top = new_top
        return top, total

    def finish(who, total):
        result[who] = (total[:, :HD] / total[:, HD:]).astype(jnp.bfloat16)

    near_lead = member // half * half
    far_lead = half - near_lead
    settle(0, half)

    @pl.loop(0, half)
    def _(step):
        who = flip(member, step, group)

        @pl.when(step > 0)
        def _():
            arrival(2, who, landings(who)[2]).wait_recv()

        pair = query_pair(who)
        top, total = absorb(pair, *start_text(pair), near_lead)
        top_kept[step] = jnp.broadcast_to(top, (query_rows, HD))
        total_kept[step] = total

    settle(half, group)

    @pl.loop(half, group)
    def _(step):
        who = flip(member, step, group)
        arrival(2, who, landings(who)[2]).wait_recv()
        pair = query_pair(who)
        top, total = absorb(pair, *start_text(pair), 0)
        top, total = absorb(pair, top, total, half)
        finish(who, total)
        remote(3, who, result.at[who], out_place(member)).start()

    @pl.loop(0, half)
    def _(place):
        step = half - 1 - place
        who = flip(member, step, group)
        top, total = absorb(query_pair(who), top_kept[step][:, :1], total_kept[step], far_lead)
        finish(who, total)

        @pl.when(step > 0)
        def _():
            remote(3, who, result.at[who], out_place(member)).start()

        @pl.when(step == 0)
        def _():
            pltpu.make_async_copy(result.at[who], out_place(member), own_sem.at[3]).start()

    pltpu.make_async_copy(result.at[member], out_place(member), own_sem.at[3]).wait()

    @pl.loop(1, group)
    def _(step):
        who = flip(member, group - step, group)
        arrival(3, who, out_place(who)).wait_recv()
        places = sources(who)
        for kind in range(3):
            remote(kind, who, places[kind], landings(member)[kind]).wait_send()
        remote(3, who, result.at[who], out_place(member)).wait_send()

    @pl.loop(1, places_here)
    def _(step):
        state_copy(flip(place, places_here - step, places_here), place).wait_send()

    @pl.loop(1, chips)
    def _(step):
        part_copy(flip(chip, chips - step, chips), chip).wait_send()

    across.wait_send()
    states_across(core).wait_send()

    for step in range(1, tp_count):
        other = flip(tp_index, step, tp_count)
        mine = terms.at[tp_index]
        transfer("tp", other, mine, mine, term_send.at[other], term_recv.at[tp_index]).wait_send()
        mine = states.at[tp_index]
        transfer("tp", other, mine, mine, side_send.at[other], side_recv.at[tp_index]).wait_send()


def local(
    llama_context,
    llama_residual,
    w_attn_out,
    w_caption,
    w_text_kv,
    prompt_length,
    image_query,
    image_key,
    image_value,
):
    sides, rows, width = image_query.shape
    heads = width // HD
    group = IMG // rows
    units = sides * heads
    seq_count = lax.axis_size("seq")
    tp_count = lax.axis_size("tp")
    seq_index = lax.axis_index("seq")
    assert group % units == 0 and CHUNK % rows == 0
    query_rows = rows * units // group
    text_rows = TXT // group
    chips = seq_count // 2
    all_rows, features = llama_residual.shape
    depth = w_caption.shape[1]
    pair_index = seq_index // group
    pair_count = prompt_length.shape[0]
    live_length = jnp.sum(
        jnp.where(jnp.arange(pair_count, dtype=jnp.int32) == pair_index, prompt_length, 0)
    )
    tokens = jnp.arange(TXT, dtype=jnp.int32).reshape(group // 2, 2, text_rows)
    tokens = tokens.transpose(1, 0, 2).reshape(TXT)
    bias = jnp.where(tokens < live_length, 0.0, -1e30)
    kinds = 4
    whole = pl.BlockSpec(memory_space=pl.ANY)
    vmem = pl.BlockSpec(memory_space=pltpu.VMEM)
    return pl.pallas_call(
        functools.partial(attend_kernel, group, sides, heads, seq_count, tp_count),
        out_shape=jax.ShapeDtypeStruct(image_query.shape, jnp.bfloat16),
        in_specs=[whole] * 8 + [vmem],
        out_specs=whole,
        scratch_shapes=[
            pltpu.VMEM(llama_context.shape, jnp.bfloat16),
            pltpu.VMEM(llama_residual.shape, jnp.bfloat16),
            pltpu.VMEM(w_attn_out.shape, jnp.bfloat16),
            pltpu.VMEM(w_caption.shape, jnp.bfloat16),
            pltpu.VMEM(w_text_kv.shape[:2] + (HD,), jnp.bfloat16),
            pltpu.VMEM((group, rows, 2 * HD), jnp.bfloat16),
            pltpu.VMEM((group, rows, 2 * HD), jnp.bfloat16),
            pltpu.VMEM((group, query_rows, HD), jnp.bfloat16),
            pltpu.VMEM((tp_count, all_rows, features), jnp.bfloat16),
            pltpu.VMEM((2, chips, text_rows, depth), jnp.bfloat16),
            pltpu.VMEM((chips, text_rows, depth), jnp.bfloat16),
            pltpu.VMEM((chips, text_rows, depth), jnp.bfloat16),
            pltpu.VMEM((chips, text_rows, depth), jnp.bfloat16),
            pltpu.VMEM((tp_count, 2, group // 2, text_rows, depth), jnp.bfloat16),
            pltpu.VMEM((TXT, 2 * HD), jnp.bfloat16),
            pltpu.VMEM((TXT, 2 * HD), jnp.bfloat16),
            pltpu.VMEM((group, query_rows, HD), jnp.bfloat16),
            pltpu.VMEM((group // 2, query_rows, HD), jnp.float32),
            pltpu.VMEM((group // 2, query_rows, 2 * HD), jnp.float32),
            pltpu.SemaphoreType.DMA((5,)),
            pltpu.SemaphoreType.DMA((4,)),
            pltpu.SemaphoreType.DMA((kinds,)),
            pltpu.SemaphoreType.DMA((kinds, group)),
            pltpu.SemaphoreType.DMA((kinds, group)),
            pltpu.SemaphoreType.DMA((tp_count,)),
            pltpu.SemaphoreType.DMA((tp_count,)),
            pltpu.SemaphoreType.DMA((chips,)),
            pltpu.SemaphoreType.DMA((chips,)),
            pltpu.SemaphoreType.DMA((group // 2,)),
            pltpu.SemaphoreType.DMA((group // 2,)),
            pltpu.SemaphoreType.DMA((tp_count,)),
            pltpu.SemaphoreType.DMA((tp_count,)),
        ],
        compiler_params=pltpu.CompilerParams(
            collective_id=0, has_side_effects=True, vmem_limit_bytes=63 * 2**20
        ),
        cost_estimate=pl.CostEstimate(
            flops=8 * image_query.size * (IMG + TXT),
            bytes_accessed=8 * image_query.size,
            transcendentals=group * query_rows * (IMG + TXT),
        ),
    )(
        image_query,
        image_key,
        image_value,
        llama_context,
        llama_residual,
        w_attn_out,
        w_caption,
        w_text_kv,
        bias.astype(jnp.float32)[None, :],
    )


def solution(mesh):
    placed = (
        P(None, "tp"),
        P(None, "seq"),
        P("tp", "seq"),
        P("seq", "tp"),
        P(None, None, "tp"),
        P(),
        P(None, "seq", "tp"),
        P(None, "seq", "tp"),
        P(None, "seq", "tp"),
    )
    return jax.shard_map(
        local, mesh=mesh, in_specs=placed, out_specs=P(None, "seq", "tp"), check_vma=False
    )
```

```python
import functools
import math

import jax
import jax.numpy as jnp
from jax import lax
from jax.experimental import pallas as pl
from jax.experimental.pallas import tpu as pltpu
from jax.sharding import PartitionSpec as P

TXT = 128
HD = 128
IMG = 4096
CHUNK = 1024
FACTOR = math.log2(math.e) / math.sqrt(HD)
NT = (((1,), (1,)), ((), ()))


def flip(index, step, count):
    result = 0
    bit = 1
    while bit < count:
        result = result + ((index // bit + step // bit) % 2) * bit
        bit *= 2
    return result


def attend_kernel(
    group,
    sides,
    heads,
    seq_count,
    tp_count,
    query,
    key,
    value,
    context_far,
    residual_far,
    w_out_far,
    w_caption_far,
    w_text_far,
    bias,
    out,
    context,
    residual,
    w_out,
    w_caption,
    w_head,
    key_land,
    value_land,
    query_land,
    terms,
    parts,
    chip_land,
    chip_parts,
    parts_land,
    states,
    text_key,
    text_value,
    result,
    top_kept,
    total_kept,
    load_sem,
    core_sem,
    own_sem,
    send_sem,
    recv_sem,
    term_send,
    term_recv,
    part_send,
    part_recv,
    state_send,
    state_recv,
    side_send,
    side_recv,
):
    units = sides * heads
    rows = query.shape[1]
    query_rows = query_land.shape[1]
    seq_index = lax.axis_index("seq")
    tp_index = lax.axis_index("tp")
    base = seq_index // group * group
    member = seq_index % group

    def unit_of(who):
        unit = who % units
        return unit // heads, unit % heads, who // units

    def columns(head):
        return pl.ds(pl.multiple_of(head * HD, HD), HD)

    core = seq_index % 2
    twin = flip(seq_index, 1, seq_count)
    chip = seq_index // 2
    chips = seq_count // 2
    head_here = unit_of(member)[1]
    loads = [
        pltpu.make_async_copy(source, target, load_sem.at[index])
        for index, (source, target) in enumerate(
            (
                (context_far, context),
                (w_out_far, w_out),
                (residual_far, residual),
                (w_caption_far, w_caption),
                (w_text_far.at[:, :, columns(head_here)], w_head),
            )
        )
    ]
    for load in loads:
        load.start()

    barrier = pltpu.get_barrier_semaphore()

    @pl.loop(1, seq_count)
    def _(step):
        pl.semaphore_signal(
            barrier,
            inc=1,
            device_id={"seq": flip(seq_index, step, seq_count)},
            device_id_type=pl.DeviceIdType.MESH,
        )

    for step in range(1, tp_count):
        pl.semaphore_signal(
            barrier,
            inc=1,
            device_id={"tp": flip(tp_index, step, tp_count)},
            device_id_type=pl.DeviceIdType.MESH,
        )
    pl.semaphore_wait(barrier, seq_count + tp_count - 2)

    def transfer(axis, who, source, target, sent, landed):
        return pltpu.make_async_remote_copy(
            src_ref=source,
            dst_ref=target,
            send_sem=sent,
            recv_sem=landed,
            device_id={axis: who},
            device_id_type=pl.DeviceIdType.MESH,
        )

    def remote(kind, who, source, target):
        return pltpu.make_async_remote_copy(
            src_ref=source,
            dst_ref=target,
            send_sem=send_sem.at[kind, who],
            recv_sem=recv_sem.at[kind, member],
            device_id={"seq": base + who},
            device_id_type=pl.DeviceIdType.MESH,
        )

    def arrival(kind, who, target):
        return pltpu.make_async_remote_copy(
            src_ref=target,
            dst_ref=target,
            send_sem=send_sem.at[kind, who],
            recv_sem=recv_sem.at[kind, who],
            device_id={"seq": base + who},
            device_id_type=pl.DeviceIdType.MESH,
        )

    def sources(who):
        side, head, part = unit_of(who)
        cols = columns(head)
        first = pl.multiple_of(part * query_rows, query_rows)
        return (
            key.at[side, :, cols],
            value.at[side, :, cols],
            query.at[side, pl.ds(first, query_rows), cols],
        )

    def landings(who):
        return (
            key_land.at[who, :, pl.ds(0, HD)],
            value_land.at[who, :, pl.ds(0, HD)],
            query_land.at[who],
        )

    def out_place(who):
        side, head, part = unit_of(who)
        first = pl.multiple_of(part * query_rows, query_rows)
        return out.at[side, pl.ds(first, query_rows), columns(head)]

    mine_from = sources(member)
    mine_to = landings(member)
    own = [
        pltpu.make_async_copy(mine_from[kind], mine_to[kind], own_sem.at[kind]) for kind in range(3)
    ]
    def send(kind, step):
        who = flip(member, step, group)
        remote(kind, who, sources(who)[kind], landings(member)[kind]).start()

    def key_wave(first, last):
        @pl.loop(first, last)
        def _(place):
            send(0, half + place)
            send(0, place + 1)
            send(1, place + 1)

    def value_wave(first, last):
        @pl.loop(first, last)
        def _(place):
            send(1, half + place)
            send(2, place + 1)

    half = group // 2
    key_wave(0, half // 2)
    for copy in own:
        copy.start()

    loads[0].wait()
    loads[1].wait()
    term = jnp.dot(context[...], w_out[...], preferred_element_type=jnp.float32)
    terms[tp_index] = term.astype(jnp.bfloat16)
    for step in range(1, tp_count):
        other = flip(tp_index, step, tp_count)
        mine = terms.at[tp_index]
        transfer("tp", other, mine, mine, term_send.at[other], term_recv.at[tp_index]).start()
    key_wave(half // 2, half - 1)
    send(0, group - 1)
    value_land[:, :, HD:] = jnp.ones((group, rows, HD), jnp.bfloat16)
    text_value[:, HD:] = jnp.ones((TXT, HD), jnp.bfloat16)
    for step in range(1, tp_count):
        other = flip(tp_index, step, tp_count)
        theirs = terms.at[other]
        transfer("tp", other, theirs, theirs, term_send.at[other], term_recv.at[other]).wait_recv()
    attended = terms[0].astype(jnp.float32)
    for index in range(1, tp_count):
        attended = attended + terms[index].astype(jnp.float32)
    loads[2].wait()
    loads[3].wait()
    hidden = (residual[...].astype(jnp.float32) + attended).astype(jnp.bfloat16)
    caption = jnp.dot(hidden, w_caption[...], preferred_element_type=jnp.float32)
    split = caption.reshape(chips, 2, parts.shape[2], parts.shape[3]).astype(jnp.bfloat16)
    parts[0] = split[:, 0]
    parts[1] = split[:, 1]
    across = transfer(
        "seq", twin, parts.at[1 - core], chip_land, core_sem.at[0], core_sem.at[1]
    )
    across.start()
    value_wave(0, half // 4)
    across.wait_recv()
    chip_parts[...] = (
        parts[core].astype(jnp.float32) + chip_land[...].astype(jnp.float32)
    ).astype(jnp.bfloat16)

    def part_copy(who, landed):
        return transfer(
            "seq",
            who * 2 + core,
            chip_parts.at[who],
            parts_land.at[landed],
            part_send.at[who],
            part_recv.at[landed],
        )

    @pl.loop(1, chips)
    def _(step):
        part_copy(flip(chip, chips - step, chips), chip).start()

    parts_land[chip] = chip_parts[chip]
    value_wave(half // 4, half // 2)

    @pl.loop(1, chips)
    def _(step):
        who = flip(chip, chips - step, chips)
        part_copy(who, who).wait_recv()

    summed = jnp.sum(parts_land[...].astype(jnp.float32), axis=0)
    place = member // 2
    places_here = group // 2
    states[tp_index, core, place] = summed.astype(jnp.bfloat16)

    def state_copy(who, owner):
        block = states.at[tp_index, core, owner]
        return transfer(
            "seq", base + who * 2 + core, block, block, state_send.at[who], state_recv.at[owner]
        )

    @pl.loop(1, places_here)
    def _(step):
        state_copy(flip(place, places_here - step, places_here), place).start()

    value_wave(half // 2, half // 2 + half // 4)

    @pl.loop(1, places_here)
    def _(step):
        who = flip(place, places_here - step, places_here)
        state_copy(who, who).wait_recv()

    def states_across(half_from):
        block = states.at[tp_index, half_from]
        return transfer("seq", twin, block, block, core_sem.at[2], core_sem.at[3])

    states_across(core).start()
    value_wave(half // 2 + half // 4, half - 1)
    send(1, group - 1)
    states_across(1 - core).wait_recv()

    for step in range(1, tp_count):
        other = flip(tp_index, step, tp_count)
        mine = states.at[tp_index]
        transfer("tp", other, mine, mine, side_send.at[other], side_recv.at[tp_index]).start()

    @pl.loop(half, group)
    def _(step):
        send(2, step)

    for step in range(1, tp_count):
        other = flip(tp_index, step, tp_count)
        theirs = states.at[other]
        transfer("tp", other, theirs, theirs, side_send.at[other], side_recv.at[other]).wait_recv()
    depth = w_caption.shape[1]
    loads[4].wait()
    text = [jnp.zeros((TXT, HD), jnp.float32) for _ in range(2)]
    for index in range(tp_count):
        block = states[index].astype(jnp.float32).reshape(TXT, depth).astype(jnp.bfloat16)
        cut = pl.ds(index * depth, depth)
        for kind in range(2):
            text[kind] = text[kind] + jnp.dot(
                block, w_head[cut, kind, :], preferred_element_type=jnp.float32
            )
    text_keys = text[0].astype(jnp.bfloat16)
    text_key[:, :HD] = text_keys
    text_key[:, HD:] = text_keys
    text_value[:, :HD] = text[1].astype(jnp.bfloat16)

    for copy in own:
        copy.wait()

    def settle(first_step, last_step):
        @pl.loop(first_step, last_step)
        def _(step):
            who = flip(member, step, group)

            @pl.when(step > 0)
            def _():
                for kind in range(2):
                    arrival(kind, who, landings(who)[kind]).wait_recv()

            key_land[who, :, HD:] = key_land[who, :, :HD]

    def query_pair(who):
        scaled = query_land[who].astype(jnp.float32) * FACTOR
        high = scaled.astype(jnp.bfloat16)
        low = (scaled - high.astype(jnp.float32)).astype(jnp.bfloat16)
        return jnp.concatenate([high, low], axis=1)

    def start_text(pair):
        scores = lax.dot_general(pair, text_key[...], NT, preferred_element_type=jnp.float32)
        scores = scores + bias[...]
        top = jnp.max(scores, axis=1, keepdims=True)
        weights = jnp.exp2(scores - top).astype(jnp.bfloat16)
        return top, jnp.dot(weights, text_value[...], preferred_element_type=jnp.float32)

    blocks = CHUNK // rows

    def absorb(pair, top, total, lead):
        for first in range(0, half, blocks):
            cut = pl.ds(lead + first, blocks)
            keys = key_land[cut].reshape(CHUNK, 2 * HD)
            values = value_land[cut].reshape(CHUNK, 2 * HD)
            scores = lax.dot_general(pair, keys, NT, preferred_element_type=jnp.float32)
            new_top = jnp.maximum(top, jnp.max(scores, axis=1, keepdims=True))
            weights = jnp.exp2(scores - new_top).astype(jnp.bfloat16)
            total = total * jnp.exp2(top - new_top) + jnp.dot(
                weights, values, preferred_element_type=jnp.float32
            )
            top = new_top
        return top, total

    def finish(who, total):
        result[who] = (total[:, :HD] / total[:, HD:]).astype(jnp.bfloat16)

    near_lead = member // half * half
    far_lead = half - near_lead
    settle(0, half)

    @pl.loop(0, half)
    def _(step):
        who = flip(member, step, group)

        @pl.when(step > 0)
        def _():
            arrival(2, who, landings(who)[2]).wait_recv()

        pair = query_pair(who)
        top, total = absorb(pair, *start_text(pair), near_lead)
        top_kept[step] = jnp.broadcast_to(top, (query_rows, HD))
        total_kept[step] = total

    settle(half, group)

    @pl.loop(half, group)
    def _(step):
        who = flip(member, step, group)
        arrival(2, who, landings(who)[2]).wait_recv()
        pair = query_pair(who)
        top, total = absorb(pair, *start_text(pair), 0)
        top, total = absorb(pair, top, total, half)
        finish(who, total)
        remote(3, who, result.at[who], out_place(member)).start()

        near = group - 1 - step
        peer = flip(member, near, group)
        top, total = absorb(query_pair(peer), top_kept[near][:, :1], total_kept[near], far_lead)
        finish(peer, total)

        @pl.when(near > 0)
        def _():
            remote(3, peer, result.at[peer], out_place(member)).start()

        @pl.when(near == 0)
        def _():
            pltpu.make_async_copy(result.at[peer], out_place(member), own_sem.at[3]).start()

    pltpu.make_async_copy(result.at[member], out_place(member), own_sem.at[3]).wait()

    @pl.loop(1, group)
    def _(step):
        who = flip(member, group - step, group)
        arrival(3, who, out_place(who)).wait_recv()
        places = sources(who)
        for kind in range(3):
            remote(kind, who, places[kind], landings(member)[kind]).wait_send()
        remote(3, who, result.at[who], out_place(member)).wait_send()

    @pl.loop(1, places_here)
    def _(step):
        state_copy(flip(place, places_here - step, places_here), place).wait_send()

    @pl.loop(1, chips)
    def _(step):
        part_copy(flip(chip, chips - step, chips), chip).wait_send()

    across.wait_send()
    states_across(core).wait_send()

    for step in range(1, tp_count):
        other = flip(tp_index, step, tp_count)
        mine = terms.at[tp_index]
        transfer("tp", other, mine, mine, term_send.at[other], term_recv.at[tp_index]).wait_send()
        mine = states.at[tp_index]
        transfer("tp", other, mine, mine, side_send.at[other], side_recv.at[tp_index]).wait_send()


def local(
    llama_context,
    llama_residual,
    w_attn_out,
    w_caption,
    w_text_kv,
    prompt_length,
    image_query,
    image_key,
    image_value,
):
    sides, rows, width = image_query.shape
    heads = width // HD
    group = IMG // rows
    units = sides * heads
    seq_count = lax.axis_size("seq")
    tp_count = lax.axis_size("tp")
    seq_index = lax.axis_index("seq")
    assert group % units == 0 and CHUNK % rows == 0
    query_rows = rows * units // group
    text_rows = TXT // group
    chips = seq_count // 2
    all_rows, features = llama_residual.shape
    depth = w_caption.shape[1]
    pair_index = seq_index // group
    pair_count = prompt_length.shape[0]
    live_length = jnp.sum(
        jnp.where(jnp.arange(pair_count, dtype=jnp.int32) == pair_index, prompt_length, 0)
    )
    tokens = jnp.arange(TXT, dtype=jnp.int32).reshape(group // 2, 2, text_rows)
    tokens = tokens.transpose(1, 0, 2).reshape(TXT)
    bias = jnp.where(tokens < live_length, 0.0, -1e30)
    kinds = 4
    whole = pl.BlockSpec(memory_space=pl.ANY)
    vmem = pl.BlockSpec(memory_space=pltpu.VMEM)
    return pl.pallas_call(
        functools.partial(attend_kernel, group, sides, heads, seq_count, tp_count),
        out_shape=jax.ShapeDtypeStruct(image_query.shape, jnp.bfloat16),
        in_specs=[whole] * 8 + [vmem],
        out_specs=whole,
        scratch_shapes=[
            pltpu.VMEM(llama_context.shape, jnp.bfloat16),
            pltpu.VMEM(llama_residual.shape, jnp.bfloat16),
            pltpu.VMEM(w_attn_out.shape, jnp.bfloat16),
            pltpu.VMEM(w_caption.shape, jnp.bfloat16),
            pltpu.VMEM(w_text_kv.shape[:2] + (HD,), jnp.bfloat16),
            pltpu.VMEM((group, rows, 2 * HD), jnp.bfloat16),
            pltpu.VMEM((group, rows, 2 * HD), jnp.bfloat16),
            pltpu.VMEM((group, query_rows, HD), jnp.bfloat16),
            pltpu.VMEM((tp_count, all_rows, features), jnp.bfloat16),
            pltpu.VMEM((2, chips, text_rows, depth), jnp.bfloat16),
            pltpu.VMEM((chips, text_rows, depth), jnp.bfloat16),
            pltpu.VMEM((chips, text_rows, depth), jnp.bfloat16),
            pltpu.VMEM((chips, text_rows, depth), jnp.bfloat16),
            pltpu.VMEM((tp_count, 2, group // 2, text_rows, depth), jnp.bfloat16),
            pltpu.VMEM((TXT, 2 * HD), jnp.bfloat16),
            pltpu.VMEM((TXT, 2 * HD), jnp.bfloat16),
            pltpu.VMEM((group, query_rows, HD), jnp.bfloat16),
            pltpu.VMEM((group // 2, query_rows, HD), jnp.float32),
            pltpu.VMEM((group // 2, query_rows, 2 * HD), jnp.float32),
            pltpu.SemaphoreType.DMA((5,)),
            pltpu.SemaphoreType.DMA((4,)),
            pltpu.SemaphoreType.DMA((kinds,)),
            pltpu.SemaphoreType.DMA((kinds, group)),
            pltpu.SemaphoreType.DMA((kinds, group)),
            pltpu.SemaphoreType.DMA((tp_count,)),
            pltpu.SemaphoreType.DMA((tp_count,)),
            pltpu.SemaphoreType.DMA((chips,)),
            pltpu.SemaphoreType.DMA((chips,)),
            pltpu.SemaphoreType.DMA((group // 2,)),
            pltpu.SemaphoreType.DMA((group // 2,)),
            pltpu.SemaphoreType.DMA((tp_count,)),
            pltpu.SemaphoreType.DMA((tp_count,)),
        ],
        compiler_params=pltpu.CompilerParams(
            collective_id=0, has_side_effects=True, vmem_limit_bytes=63 * 2**20
        ),
        cost_estimate=pl.CostEstimate(
            flops=8 * image_query.size * (IMG + TXT),
            bytes_accessed=8 * image_query.size,
            transcendentals=group * query_rows * (IMG + TXT),
        ),
    )(
        image_query,
        image_key,
        image_value,
        llama_context,
        llama_residual,
        w_attn_out,
        w_caption,
        w_text_kv,
        bias.astype(jnp.float32)[None, :],
    )


def solution(mesh):
    placed = (
        P(None, "tp"),
        P(None, "seq"),
        P("tp", "seq"),
        P("seq", "tp"),
        P(None, None, "tp"),
        P(),
        P(None, "seq", "tp"),
        P(None, "seq", "tp"),
        P(None, "seq", "tp"),
    )
    return jax.shard_map(
        local, mesh=mesh, in_specs=placed, out_specs=P(None, "seq", "tp"), check_vma=False
    )
```
